256 devices in a mesh: prow: 16 (over y, x), pcol: 16 (over z, core).
Axes of the slice: x: 4, y: 4, z: 8, core: 2. Of those that a mesh axis runs over, the one named last changes fastest.
Arguments:
- coupling: float32 [8, 2048, 8, 2048], P(None, 'prow', None, 'pcol'), as said below
- diagonal: float32 [8, 2048], P(None, 'prow'), as said below
Outputs:
- trailing: float32 [8, 2048, 8, 2048], P(None, 'prow', None, 'pcol')
Inputs may be any that keep to these rules, and one draw needn't show every extreme that they name: coupling read as in the reference program is symmetric, and coupling plus diag(diagonal) is symmetric positive definite. `diagonal`: every entry is positive.
All inputs are finite; a program needn't handle non-finite values.
Results may differ from the reference program's by a relative error of at most 0.00005.
Values sent between devices are 32-bit elements; how exact they have to be, the bound alone decides.
No kernel may reach another device: no remote copies, remote signals or barrier semaphores. Data moves between devices by JAX's collectives and lax.ppermute only.
A program may use at most 128 MiB of HBM per device.

```python
import jax
import jax.numpy as jnp
from jax import lax

NB = 128
MB = 128
N_PROW = 16
N_PCOL = 16


def row_scales(key, top):
    order = MB * NB
    base = jax.random.uniform(jax.random.fold_in(key, 11), (order,), jnp.float32)
    return jnp.exp(base * jnp.log(jnp.float32(top)))


def draw_coupling(key, part):
    scales = row_scales(key, 3.0)
    key = jax.random.fold_in(key, 1)
    order = MB * NB
    factors = jax.random.randint(key, (order, 512), -2, 3)
    factors = factors.astype(jnp.float32)
    gram = jnp.dot(factors, factors.T, precision=lax.Precision.HIGHEST)
    outer = scales[:, None] * scales[None, :]
    matrix = gram * outer * jnp.float32(0.015625)
    return matrix.reshape(MB // N_PROW, N_PROW * NB, MB // N_PCOL, N_PCOL * NB)


def draw_diagonal(key, part):
    scales = row_scales(key, 3.0)
    key = jax.random.fold_in(key, 2)
    order = MB * NB
    level = jax.random.uniform(key, (order,), jnp.float32, 2.0, 8.0)
    shift = scales * scales * level
    return shift.reshape(MB // N_PROW, N_PROW * NB)


def setup_inputs(seed: int = 0) -> dict:
    seeds = jax.random.split(jax.random.key(seed), 3)
    coupling = draw_coupling(jax.random.fold_in(seeds[2], 71), 0)
    diagonal = draw_diagonal(jax.random.fold_in(seeds[2], 71), 0)
    return {"coupling": coupling, "diagonal": diagonal}


def factor_panel(column, diag_vector, start):
    pivot = column[start:start + NB] + jnp.diag(diag_vector[start:start + NB])
    lower_factor = jnp.linalg.cholesky(pivot)
    inverse = lax.linalg.triangular_solve(lower_factor, jnp.eye(NB, dtype=jnp.float32), left_side=True, lower=True)
    below = jnp.dot(column[start + NB:], inverse.T, precision=lax.Precision.HIGHEST)
    return jnp.concatenate([jnp.zeros((start, NB), jnp.float32), lower_factor, below], axis=0)

def reference(coupling, diagonal):
    order = MB * NB
    matrix = coupling.reshape(order, order)
    diag_vector = diagonal.reshape(order)
    first = factor_panel(matrix[:, :NB], diag_vector, 0)
    column = matrix[:, NB:2 * NB] - jnp.dot(first, first[NB:2 * NB].T, precision=lax.Precision.HIGHEST)
    second = factor_panel(column, diag_vector, NB)
    updated = matrix - jnp.dot(first, first.T, precision=lax.Precision.HIGHEST)
    updated = updated - jnp.dot(second, second.T, precision=lax.Precision.HIGHEST)
    position = jnp.arange(order)
    keeping = position >= 2 * NB
    updated = jnp.where(keeping[:, None] & keeping[None, :], updated, jnp.float32(0.0))
    return updated.reshape(coupling.shape)
```

```python
import jax
import jax.numpy as jnp
from jax import lax
from jax.experimental import pallas as pl
from jax.experimental.pallas import tpu as pltpu
from jax.sharding import PartitionSpec as P

f32 = jnp.float32
bf16 = jnp.bfloat16
HIGHEST = lax.Precision.HIGHEST
AXES = ("prow", "pcol")
NT = (((1,), (1,)), ((), ()))
TN = (((0,), (0,)), ((), ()))


def place_of(row, col):
    return row % 4, row // 4, col // 2, col % 2


def send(value, target):
    pairs = []
    for row in range(16):
        for col in range(16):
            to = target(*place_of(row, col))
            if to is not None:
                x, y, z, core = to
                pairs.append((row * 16 + col, (y * 4 + x) * 16 + z * 2 + core))
    return lax.ppermute(value, AXES, pairs)


def invert_factor(rows):
    sub = lax.broadcasted_iota(jnp.int32, (8, 128), 0)
    lane = lax.broadcasted_iota(jnp.int32, (8, 128), 1)
    spread = lambda v, i: jnp.broadcast_to(v[i:i + 1, :], (8, 128))
    rows = list(rows)
    out = []
    for g in range(16):
        first = 8 * g
        column = lambda i, l: jnp.broadcast_to(rows[i][:, first + l:first + l + 1], (8, 128))
        own = [column(g, l) for l in range(8)]
        below = [[column(i, l) for l in range(8)] for i in range(g + 1, 16)]
        panel = rows[g]
        kept = jnp.zeros((8, 128), f32)
        for p in range(8):
            here = sub == p
            panel = jnp.where(lane == first + p, jnp.where(here, 1.0, 0.0), panel)
            pivot = spread(own[p], p)
            inv = 1.0 / pivot
            factor = own[p] * inv
            row = spread(panel, p)
            kept = jnp.where(here, row * lax.rsqrt(pivot), kept)
            panel = jnp.where(here, row * inv, panel - factor * row)
            for l in range(p + 1, 8):
                mine = spread(own[l], p)
                own[l] = jnp.where(here, mine * inv, own[l] - factor * mine)
        out.append(jnp.where(lane <= sub + first, kept, 0.0))
        cleared = (lane >= first) & (lane < first + 8)
        spreads = [spread(panel, l) for l in range(8)]
        for n, i in enumerate(range(g + 1, 16)):
            acc = jnp.where(cleared, 0.0, rows[i])
            for l in range(8):
                acc = acc - below[n][l] * spreads[l]
            rows[i] = acc
    return out


def exact(a, b, dims=(((1,), (0,)), ((), ()))):
    return lax.dot_general(a, b, dims, precision=HIGHEST, preferred_element_type=f32)


def groups(block):
    return [block[8 * i:8 * i + 8, :] for i in range(16)]


def factor_kernel(packed_ref, cross_ref, w_ref):
    r = lax.broadcasted_iota(jnp.int32, (128, 128), 0)
    c = lax.broadcasted_iota(jnp.int32, (128, 128), 1)
    packed = packed_ref[0:128, :]
    turned = packed.T
    s0 = jnp.where(r >= c, packed, turned)
    s1 = jnp.where(r < c, packed, jnp.where(r > c, turned, packed_ref[128:129, :]))
    w0 = jnp.concatenate(invert_factor(groups(s0)), axis=0)
    y = exact(w0, cross_ref[...])
    s1 = s1 - exact(y, y, TN)
    z = exact(y, w0, TN)
    w1 = jnp.concatenate(invert_factor(groups(s1)), axis=0)
    w_ref[0:128, 0:128] = w0
    w_ref[0:128, 128:256] = jnp.zeros((128, 128), f32)
    w_ref[128:256, 0:128] = -exact(w1, z)
    w_ref[128:256, 128:256] = w1


def factor(packed, cross):
    return pl.pallas_call(
        factor_kernel,
        out_shape=jax.ShapeDtypeStruct((256, 256), f32),
        cost_estimate=pl.CostEstimate(flops=2 * 256**3, bytes_accessed=500000, transcendentals=256),
    )(packed, cross)


def halves(x):
    high = x.astype(bf16)
    return high, (x - high.astype(f32)).astype(bf16)


def product(a, b, dims=(((1,), (0,)), ((), ()))):
    (ah, al), (bh, bl) = a, b
    dot = lambda p, q: lax.dot_general(p, q, dims, preferred_element_type=f32)
    return dot(ah, bh) + (dot(ah, bl) + dot(al, bh))


def update_kernel(place_ref, x_ref, ra_ref, rb_ref, ha_ref, hb_ref, w_ref, o_ref, out_ref, sem):
    w = halves(w_ref[...])
    cols = jnp.concatenate(
        [jnp.concatenate([h[:, c, :] for c in range(8)], axis=1) for h in (ha_ref, hb_ref)], axis=0
    )
    z = halves(product(w, halves(cols)))
    y = [
        halves(product(halves(jnp.concatenate([ra_ref[a], rb_ref[a]], axis=1)), w, NT))
        for a in range(8)
    ]
    keep_row = place_ref[0] >= 2
    keep_col = place_ref[1] >= 2
    copies = []
    for a in range(8):
        v = x_ref[a] - product(y[a], z).reshape(128, 8, 128)
        if a == 0:
            v = jnp.where(keep_row, v, 0.0)
        c = lax.broadcasted_iota(jnp.int32, v.shape, 1)
        out_ref[a] = jnp.where(jnp.logical_or(keep_col, c > 0), v, 0.0)
        copy = pltpu.make_async_copy(out_ref.at[a], o_ref.at[a], sem.at[a])
        copy.start()
        copies.append(copy)
    for copy in copies:
        copy.wait()


def update(place, x, ra, rb, ha, hb, w):
    vmem = pl.BlockSpec(memory_space=pltpu.VMEM)
    return pl.pallas_call(
        update_kernel,
        in_specs=[pl.BlockSpec(memory_space=pltpu.SMEM)] + [vmem] * 6,
        out_specs=pl.BlockSpec(memory_space=pl.ANY),
        scratch_shapes=[pltpu.VMEM((8, 128, 8, 128), f32), pltpu.SemaphoreType.DMA((8,))],
        out_shape=jax.ShapeDtypeStruct((8, 128, 8, 128), f32),
        compiler_params=pltpu.CompilerParams(vmem_limit_bytes=40 * 1024 * 1024),
        cost_estimate=pl.CostEstimate(flops=6 * 1024**2 * 256, bytes_accessed=8 * 1024**2, transcendentals=0),
    )(place, x, ra, rb, ha, hb, w)


def spread_pivots(coupling, diagonal, x, y, z, core):
    own = coupling[0, :, 0, :]
    r = lax.broadcasted_iota(jnp.int32, (128, 128), 0)
    c = lax.broadcasted_iota(jnp.int32, (128, 128), 1)
    own = own + jnp.where((r == c) & (x == core), diagonal[0][None, :], 0.0)
    moves = {(0, 0): (1, 0), (1, 1): (0, 0), (0, 1): (1, 1)}
    first = send(
        own,
        lambda x, y, z, k: (moves[x, k][0], 0, 0, moves[x, k][1]) if y == z == 0 and (x, k) in moves else None,
    )
    second = send(own, lambda x, y, z, k: (1, 0, 0, 0) if (x, y, z, k) == (1, 0, 0, 1) else None)
    s0 = jnp.where(x == 0, own, first)
    s1 = jnp.where(x == 0, first, second)
    packed = jnp.where(r >= c, s0, s1)
    packed = jnp.where(core == 0, packed, jnp.where(x == 0, own, first))
    last = jnp.sum(jnp.where(r == c, s1, 0.0), axis=0, keepdims=True)
    held = jnp.concatenate([packed, jnp.broadcast_to(last, (8, 128))], axis=0)
    held = jnp.where((y == 0) & (z == 0) & (x < 2), held, 0.0)
    held += send(held, lambda x, y, z, k: (x + 2, y, z, k) if x < 2 and y == z == 0 else None)
    held += send(held, lambda x, y, z, k: (x, y + 2, z, k) if y == z == 0 else None)
    held += send(held, lambda x, y, z, k: (x, y + 1, z, k) if y % 2 == z == 0 else None)
    held += send(held, lambda x, y, z, k: (x, y, z + 4, k) if z == 0 else None)
    held += send(held, lambda x, y, z, k: (x, y, z + 2, k) if z % 4 == 0 else None)
    held += send(held, lambda x, y, z, k: (x, y, z + 1, k) if z % 2 == 0 else None)
    other = send(held, lambda x, y, z, k: (x, y, z, 1 - k))
    return jnp.where(core == 0, held, other), jnp.where(core == 0, other, held)[0:128]


def spread_rows(coupling, x, y, z, core):
    own = jnp.where(z == 0, coupling[:, :, 0, :], 0.0)
    near = send(own, lambda x, y, z, k: (x, y, 3, k) if z == 0 else None)
    far = send(own, lambda x, y, z, k: (x, y, 5, k) if z == 0 else None)
    held = own + near + far
    up = {0: 1, 3: 4, 5: 6}
    down = {0: 7, 3: 2}
    near = send(held, lambda x, y, z, k: (x, y, up[z], k) if z in up else None)
    far = send(held, lambda x, y, z, k: (x, y, down[z], k) if z in down else None)
    held = held + near + far
    other = send(held, lambda x, y, z, k: (x, y, z, 1 - k))
    return jnp.where(core == 0, held, other), jnp.where(core == 0, other, held)


def spread_cols(coupling, x, y, z, core):
    own = coupling[0]
    held = jnp.where(y == 0, own, 0.0)
    for n in (1, 3, 2):
        held += send(own, lambda x, y, z, k: (x, n, z, k) if x < 2 and y == 0 else None)
    got = []
    for to in ({0: 1, 1: 0}, {0: 3, 1: 2}, {0: 2, 1: 3}):
        got.append(send(held, lambda x, y, z, k: (to[x], y, z, k) if x < 2 else None))
    pick = lambda n, a, b, c, d: jnp.where(n == 0, a, jnp.where(n == 1, b, jnp.where(n == 2, c, d)))
    return pick(x, held, got[0], got[2], got[1]), pick(x, got[0], held, got[1], got[2])


def on_device(coupling, diagonal):
    row = lax.axis_index("prow")
    col = lax.axis_index("pcol")
    here = place_of(row, col)
    packed, cross = spread_pivots(coupling, diagonal, *here)
    ra, rb = spread_rows(coupling, *here)
    ha, hb = spread_cols(coupling, *here)
    w = factor(packed, cross)
    place = jnp.stack([row, col]).astype(jnp.int32)
    return update(place, coupling, ra, rb, ha, hb, w)


def solution(mesh):
    return jax.shard_map(
        on_device,
        mesh=mesh,
        in_specs=(P(None, "prow", None, "pcol"), P(None, "prow")),
        out_specs=P(None, "prow", None, "pcol"),
        check_vma=False,
    )
```

```python
import jax
import jax.numpy as jnp
from jax import lax
from jax.experimental import pallas as pl
from jax.experimental.pallas import tpu as pltpu
from jax.sharding import PartitionSpec as P

f32 = jnp.float32
bf16 = jnp.bfloat16
HIGHEST = lax.Precision.HIGHEST
AXES = ("prow", "pcol")
NT = (((1,), (1,)), ((), ()))
TN = (((0,), (0,)), ((), ()))


def place_of(row, col):
    return row & 3, row >> 2, col >> 1, col & 1


def send(value, target):
    pairs = []
    for row in range(16):
        for col in range(16):
            to = target(*place_of(row, col))
            if to is not None:
                x, y, z, core = to
                pairs.append((row * 16 + col, (y * 4 + x) * 16 + z * 2 + core))
    return lax.ppermute(value, AXES, pairs)


def invert_factor(rows):
    sub = lax.broadcasted_iota(jnp.int32, (8, 128), 0)
    lane = lax.broadcasted_iota(jnp.int32, (8, 128), 1)
    spread = lambda v, i: jnp.broadcast_to(v[i:i + 1, :], (8, 128))
    rows = list(rows)
    out = []
    for g in range(16):
        first = 8 * g
        column = lambda i, l: jnp.broadcast_to(rows[i][:, first + l:first + l + 1], (8, 128))
        own = [column(g, l) for l in range(8)]
        below = [[column(i, l) for l in range(8)] for i in range(g + 1, 16)]
        panel = rows[g]
        kept = jnp.zeros((8, 128), f32)
        for p in range(8):
            here = sub == p
            panel = jnp.where(lane == first + p, jnp.where(here, 1.0, 0.0), panel)
            pivot = spread(own[p], p)
            inv = 1.0 / pivot
            factor = own[p] * inv
            row = spread(panel, p)
            kept = jnp.where(here, row * lax.rsqrt(pivot), kept)
            panel = jnp.where(here, row * inv, panel - factor * row)
            for l in range(p + 1, 8):
                mine = spread(own[l], p)
                own[l] = jnp.where(here, mine * inv, own[l] - factor * mine)
        out.append(jnp.where(lane <= sub + first, kept, 0.0))
        cleared = (lane >= first) & (lane < first + 8)
        spreads = [spread(panel, l) for l in range(8)]
        for n, i in enumerate(range(g + 1, 16)):
            acc = jnp.where(cleared, 0.0, rows[i])
            for l in range(8):
                acc = acc - below[n][l] * spreads[l]
            rows[i] = acc
    return out


def exact(a, b, dims=(((1,), (0,)), ((), ()))):
    return lax.dot_general(a, b, dims, precision=HIGHEST, preferred_element_type=f32)


def groups(block):
    return [block[8 * i:8 * i + 8, :] for i in range(16)]


def factor_kernel(core_ref, held_ref, other_ref, w_ref):
    core = core_ref[0]
    first = core == 0
    s0 = jnp.where(first, held_ref[0], other_ref[0])
    cross = jnp.where(first, other_ref[0], held_ref[0])
    s1 = jnp.where(first, other_ref[1], held_ref[1])
    w0 = jnp.concatenate(invert_factor(groups(s0)), axis=0)
    y = exact(w0, cross)
    s1 = s1 - exact(y, y, TN)
    z = exact(y, w0, TN)
    w1 = jnp.concatenate(invert_factor(groups(s1)), axis=0)
    w_ref[0:128, 0:128] = w0
    w_ref[0:128, 128:256] = jnp.zeros((128, 128), f32)
    w_ref[128:256, 0:128] = -exact(w1, z)
    w_ref[128:256, 128:256] = w1


def factor(core, held, other):
    vmem = pl.BlockSpec(memory_space=pltpu.VMEM)
    return pl.pallas_call(
        factor_kernel,
        in_specs=[pl.BlockSpec(memory_space=pltpu.SMEM), vmem, vmem],
        out_specs=vmem,
        out_shape=jax.ShapeDtypeStruct((256, 256), f32),
        cost_estimate=pl.CostEstimate(flops=2 * 256**3, bytes_accessed=500000, transcendentals=256),
    )(core, held, other)


def halves(x):
    high = x.astype(bf16)
    return high, (x - high.astype(f32)).astype(bf16)


def product(a, b, dims=(((1,), (0,)), ((), ()))):
    (ah, al), (bh, bl) = a, b
    dot = lambda p, q: lax.dot_general(p, q, dims, preferred_element_type=f32)
    return dot(ah, bh) + (dot(ah, bl) + dot(al, bh))


def update_kernel(place_ref, x_ref, held_ref, other_ref, h0_ref, h1_ref, h2_ref, h3_ref, w_ref, o_ref, out_ref, col_ref, sem):
    w = halves(w_ref[...])
    y_place = place_ref[0] // 4
    for n, h in enumerate((h0_ref, h1_ref, h2_ref, h3_ref)):
        start = pl.multiple_of(32 * lax.rem(y_place + 4 - n, 4), 32)
        for p in range(2):
            col_ref[p, pl.ds(start, 32)] = h[p]
    cols = jnp.concatenate(
        [jnp.concatenate([col_ref[p, :, c, :] for c in range(8)], axis=1) for p in range(2)], axis=0
    )
    first = lax.rem(place_ref[1], 2) == 0
    z = halves(product(w, halves(cols)))
    y = [
        halves(product(halves(jnp.concatenate(
            [jnp.where(first, held_ref[a], other_ref[a]), jnp.where(first, other_ref[a], held_ref[a])], axis=1
        )), w, NT))
        for a in range(8)
    ]
    keep_row = place_ref[0] >= 2
    keep_col = place_ref[1] >= 2
    copies = []
    for a in range(8):
        v = x_ref[a] - product(y[a], z).reshape(128, 8, 128)
        if a == 0:
            v = jnp.where(keep_row, v, 0.0)
        c = lax.broadcasted_iota(jnp.int32, v.shape, 1)
        out_ref[a] = jnp.where(jnp.logical_or(keep_col, c > 0), v, 0.0)
        copy = pltpu.make_async_copy(out_ref.at[a], o_ref.at[a], sem.at[a])
        copy.start()
        copies.append(copy)
    for copy in copies:
        copy.wait()


def update(place, x, rows, cols, w):
    vmem = pl.BlockSpec(memory_space=pltpu.VMEM)
    return pl.pallas_call(
        update_kernel,
        in_specs=[pl.BlockSpec(memory_space=pltpu.SMEM)] + [vmem] * 8,
        out_specs=pl.BlockSpec(memory_space=pl.ANY),
        scratch_shapes=[pltpu.VMEM((8, 128, 8, 128), f32), pltpu.VMEM((2, 128, 8, 128), f32), pltpu.SemaphoreType.DMA((8,))],
        out_shape=jax.ShapeDtypeStruct((8, 128, 8, 128), f32),
        compiler_params=pltpu.CompilerParams(vmem_limit_bytes=40 * 1024 * 1024),
        cost_estimate=pl.CostEstimate(flops=6 * 1024**2 * 256, bytes_accessed=8 * 1024**2, transcendentals=0),
    )(place, x, *rows, *cols, w)


def turns(values, turned):
    return [send(v, lambda x, y, z, k: (*turned(n, x, y), z, k)) for n, v in zip((1, 2, 3), values)]


def along_x(n, x, y):
    return (x + n) % 4, y


def along_y(n, x, y):
    return x, (y + n) % 4


def pick(i, options):
    out = options[3]
    for n in (2, 1, 0):
        out = jnp.where(i == n, options[n], out)
    return out


def columns_zero_and_one(own, got, x):
    ways = [own, *got]
    return jnp.stack([pick(x, ways), pick((x + 3) & 3, ways)])


def along_z(held):
    near = send(held, lambda x, y, z, k: (x, y, 3, k) if z == 0 else None)
    far = send(held, lambda x, y, z, k: (x, y, 5, k) if z == 0 else None)
    held = held + near + far
    up = {0: 1, 3: 4, 5: 6}
    down = {0: 7, 3: 2}
    near = send(held, lambda x, y, z, k: (x, y, up[z], k) if z in up else None)
    far = send(held, lambda x, y, z, k: (x, y, down[z], k) if z in down else None)
    return held + near + far


def swap(held):
    return send(held, lambda x, y, z, k: (x, y, z, 1 - k))


def spread_pivots(coupling, diagonal, x, y, z, core):
    own = coupling[0, :, 0, :]
    r = lax.broadcasted_iota(jnp.int32, (128, 128), 0)
    c = lax.broadcasted_iota(jnp.int32, (128, 128), 1)
    own = own + jnp.where((r == c) & (x == core), diagonal[0][None, :], 0.0)
    own = along_z(jnp.where(z == 0, own, 0.0))
    own = pick(y, [own, *turns([own] * 3, along_y)])
    held = columns_zero_and_one(own, turns([own] * 3, along_x), x)
    return held, swap(held)


def spread_rows(coupling, x, y, z, core):
    held = along_z(jnp.where(z == 0, coupling[:, :, 0, :], 0.0))
    return held, swap(held)


def spread_cols(coupling, x, y, z, core):
    quarters = [coupling[0, 32 * n:32 * n + 32] for n in range(4)]
    own = pick(y, [quarters[0], *turns(quarters[1:], along_y)])
    both = columns_zero_and_one(own, turns([own] * 3, along_x), x)
    return [both, *turns([both] * 3, along_y)]


def on_device(coupling, diagonal):
    row = lax.axis_index("prow")
    col = lax.axis_index("pcol")
    here = place_of(row, col)
    pivots = spread_pivots(coupling, diagonal, *here)
    rows = spread_rows(coupling, *here)
    cols = spread_cols(coupling, *here)
    place = jnp.stack([row, col]).astype(jnp.int32)
    w = factor(place[1:] & 1, *pivots)
    return update(place, coupling, rows, cols, w)


def solution(mesh):
    return jax.shard_map(
        on_device,
        mesh=mesh,
        in_specs=(P(None, "prow", None, "pcol"), P(None, "prow")),
        out_specs=P(None, "prow", None, "pcol"),
        check_vma=False,
    )
```

```python
import jax
import jax.numpy as jnp
from jax import lax
from jax.experimental import pallas as pl
from jax.experimental.pallas import tpu as pltpu
from jax.sharding import PartitionSpec as P

f32 = jnp.float32
bf16 = jnp.bfloat16
HIGHEST = lax.Precision.HIGHEST
AXES = ("prow", "pcol")
NT = (((1,), (1,)), ((), ()))
TN = (((0,), (0,)), ((), ()))


def place_of(row, col):
    return row & 3, row >> 2, col >> 1, col & 1


def send(value, target):
    pairs = []
    for row in range(16):
        for col in range(16):
            to = target(*place_of(row, col))
            if to is not None:
                x, y, z, core = to
                pairs.append((row * 16 + col, (y * 4 + x) * 16 + z * 2 + core))
    return lax.ppermute(value, AXES, pairs)


def invert_factor(rows):
    sub = lax.broadcasted_iota(jnp.int32, (8, 128), 0)
    lane = lax.broadcasted_iota(jnp.int32, (8, 128), 1)
    spread = lambda v, i: jnp.broadcast_to(v[i:i + 1, :], (8, 128))
    rows = list(rows)
    out = []
    for g in range(16):
        first = 8 * g
        column = lambda i, l: jnp.broadcast_to(rows[i][:, first + l:first + l + 1], (8, 128))
        own = [column(g, l) for l in range(8)]
        below = [[column(i, l) for l in range(8)] for i in range(g + 1, 16)]
        panel = rows[g]
        kept = jnp.zeros((8, 128), f32)
        for p in range(8):
            here = sub == p
            panel = jnp.where(lane == first + p, jnp.where(here, 1.0, 0.0), panel)
            pivot = spread(own[p], p)
            inv = 1.0 / pivot
            factor = own[p] * inv
            row = spread(panel, p)
            kept = jnp.where(here, row * lax.rsqrt(pivot), kept)
            panel = jnp.where(here, row * inv, panel - factor * row)
            for l in range(p + 1, 8):
                mine = spread(own[l], p)
                own[l] = jnp.where(here, mine * inv, own[l] - factor * mine)
        out.append(jnp.where(lane <= sub + first, kept, 0.0))
        cleared = (lane >= first) & (lane < first + 8)
        spreads = [spread(panel, l) for l in range(8)]
        for n, i in enumerate(range(g + 1, 16)):
            acc = jnp.where(cleared, 0.0, rows[i])
            for l in range(8):
                acc = acc - below[n][l] * spreads[l]
            rows[i] = acc
    return out


def exact(a, b, dims=(((1,), (0,)), ((), ()))):
    return lax.dot_general(a, b, dims, precision=HIGHEST, preferred_element_type=f32)


def groups(block):
    return [block[8 * i:8 * i + 8, :] for i in range(16)]


def factor_kernel(core_ref, held_ref, other_ref, w_ref):
    core = core_ref[0]
    first = core == 0
    s0 = jnp.where(first, held_ref[0], other_ref[0])
    cross = jnp.where(first, other_ref[0], held_ref[0])
    s1 = jnp.where(first, other_ref[1], held_ref[1])
    w0 = jnp.concatenate(invert_factor(groups(s0)), axis=0)
    y = exact(w0, cross)
    s1 = s1 - exact(y, y, TN)
    z = exact(y, w0, TN)
    w1 = jnp.concatenate(invert_factor(groups(s1)), axis=0)
    w_ref[0:128, 0:128] = w0
    w_ref[0:128, 128:256] = jnp.zeros((128, 128), f32)
    w_ref[128:256, 0:128] = -exact(w1, z)
    w_ref[128:256, 128:256] = w1


def factor(core, held, other):
    vmem = pl.BlockSpec(memory_space=pltpu.VMEM)
    return pl.pallas_call(
        factor_kernel,
        in_specs=[pl.BlockSpec(memory_space=pltpu.SMEM), vmem, vmem],
        out_specs=vmem,
        out_shape=jax.ShapeDtypeStruct((256, 256), f32),
        compiler_params=pltpu.CompilerParams(vmem_limit_bytes=8 * 1024 * 1024),
        cost_estimate=pl.CostEstimate(flops=12 * 10**9, bytes_accessed=500000, transcendentals=256),
    )(core, held, other)


def halves(x):
    high = x.astype(bf16)
    return high, (x - high.astype(f32)).astype(bf16)


def product(a, b, dims=(((1,), (0,)), ((), ()))):
    (ah, al), (bh, bl) = a, b
    dot = lambda p, q: lax.dot_general(p, q, dims, preferred_element_type=f32)
    return dot(ah, bh) + (dot(ah, bl) + dot(al, bh))


def update_kernel(place_ref, x_ref, held_ref, o0_ref, o1_ref, o2_ref, o3_ref, h0_ref, h1_ref, h2_ref, h3_ref, w_ref, o_ref, out_ref, col_ref, sem):
    w = halves(w_ref[...])
    y_place = place_ref[0] // 4
    for n, h in enumerate((h0_ref, h1_ref, h2_ref, h3_ref)):
        start = pl.multiple_of(32 * lax.rem(y_place + 4 - n, 4), 32)
        for p in range(2):
            col_ref[p, pl.ds(start, 32)] = h[p]
    cols = jnp.concatenate(
        [jnp.concatenate([col_ref[p, :, c, :] for c in range(8)], axis=1) for p in range(2)], axis=0
    )
    first = lax.rem(place_ref[1], 2) == 0
    other = [ref[n] for ref in (o0_ref, o1_ref, o2_ref, o3_ref) for n in range(2)]
    z = halves(product(w, halves(cols)))
    y = [
        halves(product(halves(jnp.concatenate(
            [jnp.where(first, held_ref[a], other[a]), jnp.where(first, other[a], held_ref[a])], axis=1
        )), w, NT))
        for a in range(8)
    ]
    keep_row = place_ref[0] >= 2
    keep_col = place_ref[1] >= 2
    copies = []
    for a in range(8):
        v = x_ref[a] - product(y[a], z).reshape(128, 8, 128)
        if a == 0:
            v = jnp.where(keep_row, v, 0.0)
        c = lax.broadcasted_iota(jnp.int32, v.shape, 1)
        out_ref[a] = jnp.where(jnp.logical_or(keep_col, c > 0), v, 0.0)
        copy = pltpu.make_async_copy(out_ref.at[a], o_ref.at[a], sem.at[a])
        copy.start()
        copies.append(copy)
    for copy in copies:
        copy.wait()


def update(place, x, rows, cols, w):
    vmem = pl.BlockSpec(memory_space=pltpu.VMEM)
    return pl.pallas_call(
        update_kernel,
        in_specs=[pl.BlockSpec(memory_space=pltpu.SMEM)] + [vmem] * 11,
        out_specs=pl.BlockSpec(memory_space=pl.ANY),
        scratch_shapes=[pltpu.VMEM((8, 128, 8, 128), f32), pltpu.VMEM((2, 128, 8, 128), f32), pltpu.SemaphoreType.DMA((8,))],
        out_shape=jax.ShapeDtypeStruct((8, 128, 8, 128), f32),
        compiler_params=pltpu.CompilerParams(vmem_limit_bytes=24 * 1024 * 1024),
        cost_estimate=pl.CostEstimate(flops=6 * 1024**2 * 256, bytes_accessed=8 * 1024**2, transcendentals=0),
    )(place, x, *rows, *cols, w)


def turns(values, turned):
    return [send(v, lambda x, y, z, k: (*turned(n, x, y), z, k)) for n, v in zip((1, 2, 3), values)]


def along_x(n, x, y):
    return (x + n) % 4, y


def along_y(n, x, y):
    return x, (y + n) % 4


def pick(i, options):
    out = options[3]
    for n in (2, 1, 0):
        out = jnp.where(i == n, options[n], out)
    return out


def columns_zero_and_one(own, got, x):
    ways = [own, *got]
    return jnp.stack([pick(x, ways), pick((x + 3) & 3, ways)])


def after(value, *others):
    return lax.optimization_barrier((value, *others))[0]


def first_z(held):
    near = send(held, lambda x, y, z, k: (x, y, 3, k) if z == 0 else None)
    far = send(held, lambda x, y, z, k: (x, y, 5, k) if z == 0 else None)
    return held, near, far


def second_z(held):
    up = {0: 1, 3: 4, 5: 6}
    down = {0: 7, 3: 2}
    near = send(held, lambda x, y, z, k: (x, y, up[z], k) if z in up else None)
    far = send(held, lambda x, y, z, k: (x, y, down[z], k) if z in down else None)
    return held, near, far


def total(parts):
    return parts[0] + parts[1] + parts[2]


def swap(held):
    return send(held, lambda x, y, z, k: (x, y, z, 1 - k))


def pivot_block(coupling, diagonal, x, core):
    own = coupling[0, :, 0, :]
    r = lax.broadcasted_iota(jnp.int32, (128, 128), 0)
    c = lax.broadcasted_iota(jnp.int32, (128, 128), 1)
    return own + jnp.where((r == c) & (x == core), diagonal[0][None, :], 0.0)


def on_device(coupling, diagonal):
    row = lax.axis_index("prow")
    col = lax.axis_index("pcol")
    x, y, z, core = place_of(row, col)
    place = jnp.stack([row, col]).astype(jnp.int32)

    pivot = jnp.where(z == 0, pivot_block(coupling, diagonal, x, core), 0.0)
    rows = jnp.where(z == 0, coupling[:, :, 0, :], 0.0)
    pivot = total(first_z(pivot))
    rows = first_z(after(rows, pivot))
    pivot = total(second_z(pivot))
    quarters = [coupling[0, 32 * n:32 * n + 32] for n in range(4)]
    cols = pick(y, [quarters[0], *turns(quarters[1:], along_y)])
    pivot = pick(y, [pivot, *turns([pivot] * 3, along_y)])
    cols = columns_zero_and_one(cols, turns([cols] * 3, along_x), x)
    pivots = columns_zero_and_one(pivot, turns([pivot] * 3, along_x), x)
    other_pivots = swap(pivots)
    rows = second_z(total(rows))
    cols = [cols, *turns([cols] * 3, along_y)]
    w = factor(place[1:] & 1, pivots, other_pivots)
    rows = total((after(rows[0], w), *rows[1:]))
    return update(place, coupling, (rows, *[swap(rows[2 * n:2 * n + 2]) for n in range(4)]), cols, w)


def solution(mesh):
    return jax.shard_map(
        on_device,
        mesh=mesh,
        in_specs=(P(None, "prow", None, "pcol"), P(None, "prow")),
        out_specs=P(None, "prow", None, "pcol"),
        check_vma=False,
    )
```

```python
import jax
import jax.numpy as jnp
from jax import lax
from jax.experimental import pallas as pl
from jax.experimental.pallas import tpu as pltpu
from jax.sharding import PartitionSpec as P

f32 = jnp.float32
bf16 = jnp.bfloat16
HIGHEST = lax.Precision.HIGHEST
AXES = ("prow", "pcol")
NT = (((1,), (1,)), ((), ()))
TN = (((0,), (0,)), ((), ()))


def place_of(row, col):
    return row & 3, row >> 2, col >> 1, col & 1


def send(value, target):
    pairs = []
    for row in range(16):
        for col in range(16):
            to = target(*place_of(row, col))
            if to is not None:
                x, y, z, core = to
                pairs.append((row * 16 + col, (y * 4 + x) * 16 + z * 2 + core))
    return lax.ppermute(value, AXES, pairs)


def invert_factor(rows):
    size = rows[0].shape[0]
    shape = (size, 128)
    sub = lax.broadcasted_iota(jnp.int32, shape, 0)
    lane = lax.broadcasted_iota(jnp.int32, shape, 1)
    spread = lambda v, i: jnp.broadcast_to(v[i:i + 1, :], shape)
    rows = list(rows)
    out = []
    for g in range(128 // size):
        first = size * g
        column = lambda i, l: jnp.broadcast_to(rows[i][:, first + l:first + l + 1], shape)
        own = [column(g, l) for l in range(size)]
        below = [column(g + 1, l) for l in range(size)] if g + 1 < 128 // size else []
        panel = rows[g]
        kept = jnp.zeros(shape, f32)
        for p in range(size):
            here = sub == p
            panel = jnp.where(lane == first + p, jnp.where(here, 1.0, 0.0), panel)
            pivot = spread(own[p], p)
            inv = 1.0 / pivot
            factor = own[p] * inv
            row = spread(panel, p)
            kept = jnp.where(here, row * lax.rsqrt(pivot), kept)
            panel = jnp.where(here, row * inv, panel - factor * row)
            for l in range(p + 1, size):
                mine = spread(own[l], p)
                own[l] = jnp.where(here, mine * inv, own[l] - factor * mine)
        out.append(jnp.where(lane <= sub + first, kept, 0.0))
        cleared = (lane >= first) & (lane < first + size)
        left = rows[g + 1:]
        if not left:
            break
        acc = jnp.where(cleared, 0.0, left[0])
        for l in range(size):
            acc = acc - below[l] * spread(panel, l)
        rows[g + 1] = acc
        if len(left) > 1:
            rest = jnp.concatenate(left[1:], axis=0)
            lanes = lax.broadcasted_iota(jnp.int32, rest.shape, 1)
            cleared = (lanes >= first) & (lanes < first + size)
            zero = jnp.zeros(shape, f32)
            right = jnp.concatenate([panel if i == g else zero for i in range(128 // size)], axis=0)
            rest = jnp.where(cleared, 0.0, rest) - jnp.dot(
                jnp.where(cleared, rest, 0.0), right, precision=HIGHEST, preferred_element_type=f32)
            for n in range(len(left) - 1):
                rows[g + 2 + n] = rest[size * n:size * n + size]
    return out


def exact(a, b, dims=(((1,), (0,)), ((), ()))):
    return lax.dot_general(a, b, dims, precision=HIGHEST, preferred_element_type=f32)


def groups(block):
    return [block[16 * i:16 * i + 16, :] for i in range(8)]


def factor_kernel(core_ref, held_ref, other_ref, w_ref):
    core = core_ref[0]
    first = core == 0
    s0 = jnp.where(first, held_ref[0], other_ref[0])
    cross = jnp.where(first, other_ref[0], held_ref[0])
    s1 = jnp.where(first, other_ref[1], held_ref[1])
    w0 = jnp.concatenate(invert_factor(groups(s0)), axis=0)
    y = exact(w0, cross)
    s1 = s1 - exact(y, y, TN)
    z = exact(y, w0, TN)
    w1 = jnp.concatenate(invert_factor(groups(s1)), axis=0)
    w_ref[0:128, 0:128] = w0
    w_ref[0:128, 128:256] = jnp.zeros((128, 128), f32)
    w_ref[128:256, 0:128] = -exact(w1, z)
    w_ref[128:256, 128:256] = w1


def factor(core, held, other):
    vmem = pl.BlockSpec(memory_space=pltpu.VMEM)
    return pl.pallas_call(
        factor_kernel,
        in_specs=[pl.BlockSpec(memory_space=pltpu.SMEM), vmem, vmem],
        out_specs=vmem,
        out_shape=jax.ShapeDtypeStruct((256, 256), f32),
        compiler_params=pltpu.CompilerParams(vmem_limit_bytes=8 * 1024 * 1024),
        cost_estimate=pl.CostEstimate(flops=12 * 10**9, bytes_accessed=500000, transcendentals=256),
    )(core, held, other)


def halves(x):
    high = x.astype(bf16)
    return high, (x - high.astype(f32)).astype(bf16)


def product(a, b, dims=(((1,), (0,)), ((), ()))):
    (ah, al), (bh, bl) = a, b
    dot = lambda p, q: lax.dot_general(p, q, dims, preferred_element_type=f32)
    return dot(ah, bh) + (dot(ah, bl) + dot(al, bh))


def update_kernel(place_ref, x_ref, held_ref, o0_ref, o1_ref, o2_ref, o3_ref, h0_ref, h1_ref, h2_ref, h3_ref, w_ref, o_ref, out_ref, col_ref, sem):
    w = halves(w_ref[...])
    y_place = place_ref[0] // 4
    for n, h in enumerate((h0_ref, h1_ref, h2_ref, h3_ref)):
        start = pl.multiple_of(32 * lax.rem(y_place + 4 - n, 4), 32)
        for p in range(2):
            col_ref[p, pl.ds(start, 32)] = h[p]
    cols = jnp.concatenate(
        [jnp.concatenate([col_ref[p, :, c, :] for c in range(8)], axis=1) for p in range(2)], axis=0
    )
    first = lax.rem(place_ref[1], 2) == 0
    other = [ref[n] for ref in (o0_ref, o1_ref, o2_ref, o3_ref) for n in range(2)]
    z = halves(product(w, halves(cols)))
    y = [
        halves(product(halves(jnp.concatenate(
            [jnp.where(first, held_ref[a], other[a]), jnp.where(first, other[a], held_ref[a])], axis=1
        )), w, NT))
        for a in range(8)
    ]
    keep_row = place_ref[0] >= 2
    keep_col = place_ref[1] >= 2
    copies = []
    for a in range(8):
        v = x_ref[a] - product(y[a], z).reshape(128, 8, 128)
        if a == 0:
            v = jnp.where(keep_row, v, 0.0)
        c = lax.broadcasted_iota(jnp.int32, v.shape, 1)
        out_ref[a] = jnp.where(jnp.logical_or(keep_col, c > 0), v, 0.0)
        copy = pltpu.make_async_copy(out_ref.at[a], o_ref.at[a], sem.at[a])
        copy.start()
        copies.append(copy)
    for copy in copies:
        copy.wait()


def update(place, x, rows, cols, w):
    vmem = pl.BlockSpec(memory_space=pltpu.VMEM)
    return pl.pallas_call(
        update_kernel,
        in_specs=[pl.BlockSpec(memory_space=pltpu.SMEM)] + [vmem] * 11,
        out_specs=pl.BlockSpec(memory_space=pl.ANY),
        scratch_shapes=[pltpu.VMEM((8, 128, 8, 128), f32), pltpu.VMEM((2, 128, 8, 128), f32), pltpu.SemaphoreType.DMA((8,))],
        out_shape=jax.ShapeDtypeStruct((8, 128, 8, 128), f32),
        compiler_params=pltpu.CompilerParams(vmem_limit_bytes=24 * 1024 * 1024),
        cost_estimate=pl.CostEstimate(flops=6 * 1024**2 * 256, bytes_accessed=8 * 1024**2, transcendentals=0),
    )(place, x, *rows, *cols, w)


def turns(values, turned):
    return [send(v, lambda x, y, z, k: (*turned(n, x, y), z, k)) for n, v in zip((1, 2, 3), values)]


def along_x(n, x, y):
    return (x + n) % 4, y


def along_y(n, x, y):
    return x, (y + n) % 4


def pick(i, options):
    out = options[3]
    for n in (2, 1, 0):
        out = jnp.where(i == n, options[n], out)
    return out


def columns_zero_and_one(own, got, x):
    ways = [own, *got]
    return jnp.stack([pick(x, ways), pick((x + 3) & 3, ways)])


def after(value, *others):
    return lax.optimization_barrier((value, *others))[0]


def along_z(step, held):
    moves = ({0: 2}, {0: 6, 2: 4}, {0: 1, 2: 3, 4: 5, 6: 7})[step - 1]

    def target(x, y, z, k):
        turned = z if k == 0 else -z & 7
        if turned not in moves:
            return None
        to = moves[turned]
        return x, y, to if k == 0 else -to & 7, k

    return held, send(held, target)


def total(parts):
    return parts[0] + parts[1]


def swap(held):
    return send(held, lambda x, y, z, k: (x, y, z, 1 - k))


def pivot_block(coupling, diagonal, x, core):
    own = coupling[0, :, 0, :]
    r = lax.broadcasted_iota(jnp.int32, (128, 128), 0)
    c = lax.broadcasted_iota(jnp.int32, (128, 128), 1)
    return own + jnp.where((r == c) & (x == core), diagonal[0][None, :], 0.0)


def on_device(coupling, diagonal):
    row = lax.axis_index("prow")
    col = lax.axis_index("pcol")
    x, y, z, core = place_of(row, col)
    place = jnp.stack([row, col]).astype(jnp.int32)

    rows = jnp.where(z == 0, coupling[:, :, 0, :], 0.0)
    pivot = pivot_block(coupling, diagonal, x, core)
    quarters = [coupling[0, 32 * n:32 * n + 32] for n in range(4)]
    turned = turns([pivot] * 3, along_y)
    pivot, rows = lax.optimization_barrier((pivot, rows))
    pivot = pick(y, [pivot, *turned])
    cols = pick(y, [quarters[0], *turns(quarters[1:], along_y)])
    pivots = columns_zero_and_one(pivot, turns([pivot] * 3, along_x), x)
    rows = along_z(1, after(rows, pivots))
    pivots = total(along_z(1, jnp.where(z == 0, pivots, 0.0)))
    rows = along_z(2, after(total(rows), pivots))
    pivots, cols = lax.optimization_barrier((pivots, cols))
    cols = columns_zero_and_one(cols, turns([cols] * 3, along_x), x)
    pivots = total(along_z(2, pivots))
    pivots = total(along_z(3, pivots))
    other_pivots = swap(pivots)
    rows = along_z(3, after(total(rows), pivots))
    cols = [cols, *turns([cols] * 3, along_y)]
    w = factor(place[1:] & 1, pivots, other_pivots)
    rows = total((after(rows[0], w), rows[1]))
    return update(place, coupling, (rows, *[swap(rows[2 * n:2 * n + 2]) for n in range(4)]), cols, w)


def solution(mesh):
    return jax.shard_map(
        on_device,
        mesh=mesh,
        in_specs=(P(None, "prow", None, "pcol"), P(None, "prow")),
        out_specs=P(None, "prow", None, "pcol"),
        check_vma=False,
    )
```

```python
import jax
import jax.numpy as jnp
from jax import lax
from jax.experimental import pallas as pl
from jax.experimental.pallas import tpu as pltpu
from jax.sharding import PartitionSpec as P

f32 = jnp.float32
bf16 = jnp.bfloat16
HIGHEST = lax.Precision.HIGHEST
AXES = ("prow", "pcol")
NT = (((1,), (1,)), ((), ()))
TN = (((0,), (0,)), ((), ()))


def place_of(row, col):
    return row & 3, row >> 2, col >> 1, col & 1


def send(value, target):
    pairs = []
    for row in range(16):
        for col in range(16):
            to = target(*place_of(row, col))
            if to is not None:
                x, y, z, core = to
                pairs.append((row * 16 + col, (y * 4 + x) * 16 + z * 2 + core))
    return lax.ppermute(value, AXES, pairs)


def invert_factor(rows):
    size = rows[0].shape[0]
    shape = (size, 128)
    sub = lax.broadcasted_iota(jnp.int32, shape, 0)
    lane = lax.broadcasted_iota(jnp.int32, shape, 1)
    spread = lambda v, i: jnp.broadcast_to(v[i:i + 1, :], shape)
    rows = list(rows)
    out = []
    for g in range(128 // size):
        first = size * g
        column = lambda i, l: jnp.broadcast_to(rows[i][:, first + l:first + l + 1], shape)
        own = [column(g, l) for l in range(size)]
        below = [column(g + 1, l) for l in range(size)] if g + 1 < 128 // size else []
        panel = rows[g]
        kept = jnp.zeros(shape, f32)
        for p in range(size):
            here = sub == p
            panel = jnp.where(lane == first + p, jnp.where(here, 1.0, 0.0), panel)
            pivot = spread(own[p], p)
            inv = 1.0 / pivot
            factor = own[p] * inv
            row = spread(panel, p)
            kept = jnp.where(here, row * lax.rsqrt(pivot), kept)
            panel = jnp.where(here, row * inv, panel - factor * row)
            for l in range(p + 1, size):
                mine = spread(own[l], p)
                own[l] = jnp.where(here, mine * inv, own[l] - factor * mine)
        out.append(jnp.where(lane <= sub + first, kept, 0.0))
        cleared = (lane >= first) & (lane < first + size)
        left = rows[g + 1:]
        if not left:
            break
        acc = jnp.where(cleared, 0.0, left[0])
        for l in range(size):
            acc = acc - below[l] * spread(panel, l)
        rows[g + 1] = acc
        if len(left) > 1:
            rest = jnp.concatenate(left[1:], axis=0)
            lanes = lax.broadcasted_iota(jnp.int32, rest.shape, 1)
            cleared = (lanes >= first) & (lanes < first + size)
            zero = jnp.zeros(shape, f32)
            right = jnp.concatenate([panel if i == g else zero for i in range(128 // size)], axis=0)
            rest = jnp.where(cleared, 0.0, rest) - jnp.dot(
                jnp.where(cleared, rest, 0.0), right, precision=HIGHEST, preferred_element_type=f32)
            for n in range(len(left) - 1):
                rows[g + 2 + n] = rest[size * n:size * n + size]
    return out


def exact(a, b, dims=(((1,), (0,)), ((), ()))):
    return lax.dot_general(a, b, dims, precision=HIGHEST, preferred_element_type=f32)


def groups(block):
    return [block[16 * i:16 * i + 16, :] for i in range(8)]


def factor_kernel(core_ref, held_ref, other_ref, w_ref):
    core = core_ref[0]
    first = core == 0
    s0 = jnp.where(first, held_ref[0], other_ref[0])
    cross = jnp.where(first, other_ref[0], held_ref[0])
    s1 = jnp.where(first, other_ref[1], held_ref[1])
    w0 = jnp.concatenate(invert_factor(groups(s0)), axis=0)
    y = exact(w0, cross)
    s1 = s1 - exact(y, y, TN)
    z = exact(y, w0, TN)
    w1 = jnp.concatenate(invert_factor(groups(s1)), axis=0)
    w_ref[0:128, 0:128] = w0
    w_ref[0:128, 128:256] = jnp.zeros((128, 128), f32)
    w_ref[128:256, 0:128] = -exact(w1, z)
    w_ref[128:256, 128:256] = w1


def factor(core, held, other):
    vmem = pl.BlockSpec(memory_space=pltpu.VMEM)
    return pl.pallas_call(
        factor_kernel,
        in_specs=[pl.BlockSpec(memory_space=pltpu.SMEM), vmem, vmem],
        out_specs=vmem,
        out_shape=jax.ShapeDtypeStruct((256, 256), f32),
        compiler_params=pltpu.CompilerParams(vmem_limit_bytes=8 * 1024 * 1024),
        cost_estimate=pl.CostEstimate(flops=12 * 10**9, bytes_accessed=500000, transcendentals=256),
    )(core, held, other)


def halves(x):
    high = x.astype(bf16)
    return high, (x - high.astype(f32)).astype(bf16)


def product(a, b, dims=(((1,), (0,)), ((), ()))):
    (ah, al), (bh, bl) = a, b
    dot = lambda p, q: lax.dot_general(p, q, dims, preferred_element_type=f32)
    return dot(ah, bh) + (dot(ah, bl) + dot(al, bh))


def update_kernel(place_ref, x_ref, r0_ref, r1_ref, o0_ref, o1_ref, o2_ref, o3_ref, h0_ref, h1_ref, h2_ref, h3_ref, w_ref, o_ref, out_ref, col_ref, sem):
    w = halves(w_ref[...])
    y_place = place_ref[0] // 4
    for n, h in enumerate((h0_ref, h1_ref, h2_ref, h3_ref)):
        start = pl.multiple_of(32 * lax.rem(y_place + 4 - n, 4), 32)
        for p in range(2):
            col_ref[p, pl.ds(start, 32)] = h[p]
    cols = jnp.concatenate(
        [jnp.concatenate([col_ref[p, :, c, :] for c in range(8)], axis=1) for p in range(2)], axis=0
    )
    first = lax.rem(place_ref[1], 2) == 0
    held = [ref[n] for ref in (r0_ref, r1_ref) for n in range(4)]
    other = [ref[n] for ref in (o0_ref, o1_ref, o2_ref, o3_ref) for n in range(2)]
    z = halves(product(w, halves(cols)))
    y = [
        halves(product(halves(jnp.concatenate(
            [jnp.where(first, held[a], other[a]), jnp.where(first, other[a], held[a])], axis=1
        )), w, NT))
        for a in range(8)
    ]
    keep_row = place_ref[0] >= 2
    keep_col = place_ref[1] >= 2
    copies = []
    for a in range(8):
        v = x_ref[a] - product(y[a], z).reshape(128, 8, 128)
        if a == 0:
            v = jnp.where(keep_row, v, 0.0)
        c = lax.broadcasted_iota(jnp.int32, v.shape, 1)
        out_ref[a] = jnp.where(jnp.logical_or(keep_col, c > 0), v, 0.0)
        copy = pltpu.make_async_copy(out_ref.at[a], o_ref.at[a], sem.at[a])
        copy.start()
        copies.append(copy)
    for copy in copies:
        copy.wait()


def update(place, x, rows, cols, w):
    vmem = pl.BlockSpec(memory_space=pltpu.VMEM)
    return pl.pallas_call(
        update_kernel,
        in_specs=[pl.BlockSpec(memory_space=pltpu.SMEM)] + [vmem] * 12,
        out_specs=pl.BlockSpec(memory_space=pl.ANY),
        scratch_shapes=[pltpu.VMEM((8, 128, 8, 128), f32), pltpu.VMEM((2, 128, 8, 128), f32), pltpu.SemaphoreType.DMA((8,))],
        out_shape=jax.ShapeDtypeStruct((8, 128, 8, 128), f32),
        compiler_params=pltpu.CompilerParams(vmem_limit_bytes=24 * 1024 * 1024),
        cost_estimate=pl.CostEstimate(flops=6 * 1024**2 * 256, bytes_accessed=8 * 1024**2, transcendentals=0),
    )(place, x, *rows, *cols, w)


def turns(values, turned):
    return [send(v, lambda x, y, z, k: (*turned(n, x, y), z, k)) for n, v in zip((1, 2, 3), values)]


def along_x(n, x, y):
    return (x + n) % 4, y


def along_y(n, x, y):
    return x, (y + n) % 4


def pick(i, options):
    out = options[3]
    for n in (2, 1, 0):
        out = jnp.where(i == n, options[n], out)
    return out


def columns_zero_and_one(own, got, x):
    ways = [own, *got]
    return jnp.stack([pick(x, ways), pick((x + 3) & 3, ways)])


def after(value, *others):
    return lax.optimization_barrier((value, *others))[0]


def along_z(step, held):
    moves = ({0: 2}, {0: 6, 2: 4}, {0: 1, 2: 3, 4: 5, 6: 7})[step - 1]

    def target(x, y, z, k):
        turned = z if k == 0 else -z & 7
        if turned not in moves:
            return None
        to = moves[turned]
        return x, y, to if k == 0 else -to & 7, k

    return held, send(held, target)


def total(parts):
    return parts[0] + parts[1]


def swap(held):
    return send(held, lambda x, y, z, k: (x, y, z, 1 - k))


def pivot_block(coupling, diagonal, x, core):
    own = coupling[0, :, 0, :]
    r = lax.broadcasted_iota(jnp.int32, (128, 128), 0)
    c = lax.broadcasted_iota(jnp.int32, (128, 128), 1)
    return own + jnp.where((r == c) & (x == core), diagonal[0][None, :], 0.0)


def on_device(coupling, diagonal):
    row = lax.axis_index("prow")
    col = lax.axis_index("pcol")
    x, y, z, core = place_of(row, col)
    place = jnp.stack([row, col]).astype(jnp.int32)

    rows = jnp.where(z == 0, coupling[:, :, 0, :], 0.0)
    pivot = pivot_block(coupling, diagonal, x, core)
    quarters = [coupling[0, 32 * n:32 * n + 32] for n in range(4)]
    turned = [
        send(pivot, lambda x, y, z, k: (x, n, z, k) if x < 2 and y == z == 0 else None) for n in (1, 2, 3)
    ]
    pivot, rows = lax.optimization_barrier((pivot, rows))
    pivot = pick(y, [pivot, *turned])
    cols = pick(y, [quarters[0], *turns(quarters[1:], along_y)])
    turned = [
        send(pivot, lambda x, y, z, k: ((x + n) & 3, y, z, k) if x < 2 and z == 0 else None)
        for n in (1, 2, 3)
    ]
    pivots = columns_zero_and_one(pivot, turned, x)
    rows = along_z(1, after(rows, pivots))
    pivots = total(along_z(1, jnp.where(z == 0, pivots, 0.0)))
    rows = along_z(2, after(total(rows), pivots))
    pivots, cols = lax.optimization_barrier((pivots, cols))
    cols = columns_zero_and_one(cols, turns([cols] * 3, along_x), x)
    pivots = total(along_z(2, pivots))
    pivots = total(along_z(3, pivots))
    other_pivots = swap(pivots)
    rows = after(total(rows), pivots)
    rows = [along_z(3, half) for half in (rows[0:4], rows[4:8])]
    cols = [cols, *turns([cols] * 3, along_y)]
    w = factor(place[1:] & 1, pivots, other_pivots)
    rows = [total((after(held, w), got)) for held, got in rows]
    others = [swap(half[2 * n:2 * n + 2]) for half in rows for n in range(2)]
    return update(place, coupling, (*rows, *others), cols, w)


def solution(mesh):
    return jax.shard_map(
        on_device,
        mesh=mesh,
        in_specs=(P(None, "prow", None, "pcol"), P(None, "prow")),
        out_specs=P(None, "prow", None, "pcol"),
        check_vma=False,
    )
```

```python
import jax
import jax.numpy as jnp
from jax import lax
from jax.experimental import pallas as pl
from jax.experimental.pallas import tpu as pltpu
from jax.sharding import PartitionSpec as P

f32 = jnp.float32
bf16 = jnp.bfloat16
HIGHEST = lax.Precision.HIGHEST
AXES = ("prow", "pcol")
NT = (((1,), (1,)), ((), ()))
TN = (((0,), (0,)), ((), ()))


def place_of(row, col):
    return row & 3, row >> 2, col >> 1, col & 1


def send(value, target):
    pairs = []
    for row in range(16):
        for col in range(16):
            to = target(*place_of(row, col))
            if to is not None:
                x, y, z, core = to
                pairs.append((row * 16 + col, (y * 4 + x) * 16 + z * 2 + core))
    return lax.ppermute(value, AXES, pairs)


def invert_factor(rows):
    size = rows[0].shape[0]
    shape = (size, 128)
    sub = lax.broadcasted_iota(jnp.int32, shape, 0)
    lane = lax.broadcasted_iota(jnp.int32, shape, 1)
    spread = lambda v, i: jnp.broadcast_to(v[i:i + 1, :], shape)
    rows = list(rows)
    out = []
    for g in range(128 // size):
        first = size * g
        column = lambda i, l: jnp.broadcast_to(rows[i][:, first + l:first + l + 1], shape)
        own = [column(g, l) for l in range(size)]
        below = [column(g + 1, l) for l in range(size)] if g + 1 < 128 // size else []
        panel = rows[g]
        kept = jnp.zeros(shape, f32)
        for p in range(size):
            here = sub == p
            panel = jnp.where(lane == first + p, jnp.where(here, 1.0, 0.0), panel)
            pivot = spread(own[p], p)
            inv = 1.0 / pivot
            factor = own[p] * inv
            row = spread(panel, p)
            kept = jnp.where(here, row * lax.rsqrt(pivot), kept)
            panel = jnp.where(here, row * inv, panel - factor * row)
            for l in range(p + 1, size):
                mine = spread(own[l], p)
                own[l] = jnp.where(here, mine * inv, own[l] - factor * mine)
        out.append(jnp.where(lane <= sub + first, kept, 0.0))
        cleared = (lane >= first) & (lane < first + size)
        left = rows[g + 1:]
        if not left:
            break
        acc = jnp.where(cleared, 0.0, left[0])
        for l in range(size):
            acc = acc - below[l] * spread(panel, l)
        rows[g + 1] = acc
        if len(left) > 1:
            rest = jnp.concatenate(left[1:], axis=0)
            lanes = lax.broadcasted_iota(jnp.int32, rest.shape, 1)
            cleared = (lanes >= first) & (lanes < first + size)
            zero = jnp.zeros(shape, f32)
            right = jnp.concatenate([panel if i == g else zero for i in range(128 // size)], axis=0)
            rest = jnp.where(cleared, 0.0, rest) - jnp.dot(
                jnp.where(cleared, rest, 0.0), right, precision=HIGHEST, preferred_element_type=f32)
            for n in range(len(left) - 1):
                rows[g + 2 + n] = rest[size * n:size * n + size]
    return out


def exact(a, b, dims=(((1,), (0,)), ((), ()))):
    return lax.dot_general(a, b, dims, precision=HIGHEST, preferred_element_type=f32)


def groups(block):
    return [block[16 * i:16 * i + 16, :] for i in range(8)]


def factor_kernel(core_ref, held_ref, other_ref, w_ref):
    core = core_ref[0]
    first = core == 0
    s0 = jnp.where(first, held_ref[0], other_ref[0])
    cross = jnp.where(first, other_ref[0], held_ref[0])
    s1 = jnp.where(first, other_ref[1], held_ref[1])
    w0 = jnp.concatenate(invert_factor(groups(s0)), axis=0)
    y = exact(w0, cross)
    s1 = s1 - exact(y, y, TN)
    z = exact(y, w0, TN)
    w1 = jnp.concatenate(invert_factor(groups(s1)), axis=0)
    w_ref[0:128, 0:128] = w0
    w_ref[0:128, 128:256] = jnp.zeros((128, 128), f32)
    w_ref[128:256, 0:128] = -exact(w1, z)
    w_ref[128:256, 128:256] = w1


def factor(core, held, other):
    vmem = pl.BlockSpec(memory_space=pltpu.VMEM)
    return pl.pallas_call(
        factor_kernel,
        in_specs=[pl.BlockSpec(memory_space=pltpu.SMEM), vmem, vmem],
        out_specs=vmem,
        out_shape=jax.ShapeDtypeStruct((256, 256), f32),
        compiler_params=pltpu.CompilerParams(vmem_limit_bytes=8 * 1024 * 1024),
        cost_estimate=pl.CostEstimate(flops=12 * 10**9, bytes_accessed=500000, transcendentals=256),
    )(core, held, other)


def halves(x):
    high = x.astype(bf16)
    return high, (x - high.astype(f32)).astype(bf16)


def product(a, b, dims=(((1,), (0,)), ((), ()))):
    (ah, al), (bh, bl) = a, b
    dot = lambda p, q: lax.dot_general(p, q, dims, preferred_element_type=f32)
    return dot(ah, bh) + (dot(ah, bl) + dot(al, bh))


def update_kernel(place_ref, x_ref, r0_ref, r1_ref, o0_ref, o1_ref, h0_ref, h1_ref, h2_ref, h3_ref, w_ref, o_ref, out_ref, col_ref, sem):
    w = halves(w_ref[...])
    y_place = place_ref[0] // 4
    for n, h in enumerate((h0_ref, h1_ref, h2_ref, h3_ref)):
        start = pl.multiple_of(32 * lax.rem(y_place + 4 - n, 4), 32)
        for p in range(2):
            col_ref[p, pl.ds(start, 32)] = h[p]
    cols = jnp.concatenate(
        [jnp.concatenate([col_ref[p, :, c, :] for c in range(8)], axis=1) for p in range(2)], axis=0
    )
    first = lax.rem(place_ref[1], 2) == 0
    held = [ref[n] for ref in (r0_ref, r1_ref) for n in range(4)]
    other = [ref[n] for ref in (o0_ref, o1_ref) for n in range(4)]
    z = halves(product(w, halves(cols)))
    y = [
        halves(product(halves(jnp.concatenate(
            [jnp.where(first, held[a], other[a]), jnp.where(first, other[a], held[a])], axis=1
        )), w, NT))
        for a in range(8)
    ]
    keep_row = place_ref[0] >= 2
    keep_col = place_ref[1] >= 2
    copies = []
    for a in range(8):
        v = x_ref[a] - product(y[a], z).reshape(128, 8, 128)
        if a == 0:
            v = jnp.where(keep_row, v, 0.0)
        c = lax.broadcasted_iota(jnp.int32, v.shape, 1)
        out_ref[a] = jnp.where(jnp.logical_or(keep_col, c > 0), v, 0.0)
        copy = pltpu.make_async_copy(out_ref.at[a], o_ref.at[a], sem.at[a])
        copy.start()
        copies.append(copy)
    for copy in copies:
        copy.wait()


def update(place, x, rows, cols, w):
    vmem = pl.BlockSpec(memory_space=pltpu.VMEM)
    return pl.pallas_call(
        update_kernel,
        in_specs=[pl.BlockSpec(memory_space=pltpu.SMEM)] + [vmem] * 10,
        out_specs=pl.BlockSpec(memory_space=pl.ANY),
        scratch_shapes=[pltpu.VMEM((8, 128, 8, 128), f32), pltpu.VMEM((2, 128, 8, 128), f32), pltpu.SemaphoreType.DMA((8,))],
        out_shape=jax.ShapeDtypeStruct((8, 128, 8, 128), f32),
        compiler_params=pltpu.CompilerParams(vmem_limit_bytes=24 * 1024 * 1024),
        cost_estimate=pl.CostEstimate(flops=6 * 1024**2 * 256, bytes_accessed=8 * 1024**2, transcendentals=0),
    )(place, x, *rows, *cols, w)


def turns(values, turned):
    return [send(v, lambda x, y, z, k: (*turned(n, x, y), z, k)) for n, v in zip((1, 2, 3), values)]


def along_x(n, x, y):
    return (x + n) % 4, y


def along_y(n, x, y):
    return x, (y + n) % 4


def pick(i, options):
    out = options[3]
    for n in (2, 1, 0):
        out = jnp.where(i == n, options[n], out)
    return out


def columns_zero_and_one(own, got, x):
    ways = [own, *got]
    return jnp.stack([pick(x, ways), pick((x + 3) & 3, ways)])


def after(value, *others):
    return lax.optimization_barrier((value, *others))[0]


def along_z(step, held):
    moves = ({0: 2}, {0: 6, 2: 4}, {0: 1, 2: 3, 4: 5, 6: 7})[step - 1]

    def target(x, y, z, k):
        turned = z if k == 0 else -z & 7
        if turned not in moves:
            return None
        to = moves[turned]
        return x, y, to if k == 0 else -to & 7, k

    return held, send(held, target)


def total(parts):
    return parts[0] + parts[1]


def swap(held):
    return send(held, lambda x, y, z, k: (x, y, z, 1 - k))


def pivot_block(coupling, diagonal, x, core):
    own = coupling[0, :, 0, :]
    r = lax.broadcasted_iota(jnp.int32, (128, 128), 0)
    c = lax.broadcasted_iota(jnp.int32, (128, 128), 1)
    return own + jnp.where((r == c) & (x == core), diagonal[0][None, :], 0.0)


def on_device(coupling, diagonal):
    row = lax.axis_index("prow")
    col = lax.axis_index("pcol")
    x, y, z, core = place_of(row, col)
    place = jnp.stack([row, col]).astype(jnp.int32)

    rows = jnp.where(z == 0, coupling[:, :, 0, :], 0.0)
    pivot = pivot_block(coupling, diagonal, x, core)
    quarters = [coupling[0, 32 * n:32 * n + 32] for n in range(4)]
    turned = [
        send(pivot, lambda x, y, z, k: (x, n, z, k) if x < 2 and y == z == 0 else None) for n in (1, 2, 3)
    ]
    pivot, rows = lax.optimization_barrier((pivot, rows))
    pivot = pick(y, [pivot, *turned])
    cols = pick(y, [quarters[0], *turns(quarters[1:], along_y)])
    turned = [
        send(pivot, lambda x, y, z, k: ((x + n) & 3, y, z, k) if x < 2 and z == 0 else None)
        for n in (1, 2, 3)
    ]
    pivots = columns_zero_and_one(pivot, turned, x)
    rows = along_z(1, after(rows, pivots))
    pivots = total(along_z(1, jnp.where(z == 0, pivots, 0.0)))
    rows = along_z(2, after(total(rows), pivots))
    pivots, cols = lax.optimization_barrier((pivots, cols))
    cols = columns_zero_and_one(cols, turns([cols] * 3, along_x), x)
    pivots = total(along_z(2, pivots))
    pivots = total(along_z(3, pivots))
    other_pivots = swap(pivots)
    rows = after(total(rows), pivots)
    rows = [along_z(3, half) for half in (rows[0:4], rows[4:8])]
    cols = [cols, *turns([cols] * 3, along_y)]
    w = factor(place[1:] & 1, pivots, other_pivots)
    rows = [total((after(held, w), got)) for held, got in rows]
    others = [swap(half) for half in rows]
    return update(place, coupling, (*rows, *others), cols, w)


def solution(mesh):
    return jax.shard_map(
        on_device,
        mesh=mesh,
        in_specs=(P(None, "prow", None, "pcol"), P(None, "prow")),
        out_specs=P(None, "prow", None, "pcol"),
        check_vma=False,
    )
```
